32 devices in a mesh: segment: 2 (over x), seq: 4 (over z), mp: 4 (over y, core).
Axes of the slice: x: 2, y: 2, z: 4, core: 2. Of those that a mesh axis runs over, the one named last changes fastest.
Arguments:
- memory: bfloat16 [2, 1024, 4096], P(None, 'seq', 'mp')
- decoder_rows: bfloat16 [2, 256, 4096], P(None, 'seq', 'mp')
- gains: bfloat16 [2, 4096], P('segment'), may hold values from 0.5 to 1.5
- weights: bfloat16 [2, 2, 4096, 4096], P('segment', None, None, 'mp')
- lengths: int32 [2], replicated, may hold values from 128 to 1024, as said below
Outputs:
- decoder_out: bfloat16 [2, 256, 4096], P(None, 'seq', ('segment', 'mp'))
The draws below stay inside these ranges and needn't reach their ends.
Inputs may be any that keep to these rules, and one draw needn't show every extreme that they name: memory positions of document b at or beyond lengths[b] are padding; some document has all 1024 positions.
All inputs are finite; a program needn't handle non-finite values.
Results may differ from the reference program's by a relative error of at most 0.015.
The reference program's roundings to bfloat16 on the way count: a program that leaves them out, or rounds other values in their place, can miss the bound.
Values may be sent and summed in bfloat16 or wider, within the bound.
No kernel may reach another device: no remote copies, remote signals or barrier semaphores. Data moves between devices by JAX's collectives and lax.ppermute only.
A program may use at most 192 MiB of HBM per device.

```python
import math
import jax
import jax.numpy as jnp
from jax import lax

D = 4096
HEADS = 64
DKV = 64
DOCS = 2
HD = 4096
MEM = 1024
LEN = 256


def draw_both_rows(key):
    rows_key = jax.random.fold_in(key, 17)
    mem_key, dec_key = jax.random.split(rows_key, 2)
    memory = jax.random.normal(mem_key, (DOCS, MEM, D), jnp.float32)
    decoder = jax.random.normal(dec_key, (DOCS, LEN, D), jnp.float32)
    return (memory.astype(jnp.bfloat16), decoder.astype(jnp.bfloat16))


def draw_memory(key, part):
    return draw_both_rows(key)[0]


def draw_decoder_rows(key, part):
    return draw_both_rows(key)[1]


def draw_weights(key, part):
    raw = jax.random.normal(key, (2, 2, D, HD), jnp.float32)
    pair_scale = math.sqrt(3.0 / (D * math.sqrt(DKV)))
    key_weight = raw[0, 0] * pair_scale
    value_weight = raw[0, 1] / math.sqrt(D)
    query_weight = raw[1, 0] * pair_scale
    out_weight = raw[1, 1] * 3.0 / math.sqrt(HD)
    stacked = jnp.stack([jnp.stack([key_weight, value_weight]), jnp.stack([query_weight, out_weight])])
    return stacked.astype(jnp.bfloat16)


def draw_lengths(key, part):
    lowest = max(1, MEM // 8)
    draw_key, full_key = jax.random.split(key)
    drawn = jax.random.randint(draw_key, (DOCS,), lowest, MEM + 1)
    full_doc = jax.random.randint(full_key, (), 0, DOCS)
    return jnp.where(jnp.arange(DOCS) == full_doc, MEM, drawn).astype(jnp.int32)


def setup_inputs(seed: int = 0) -> dict:
    streams_of = jax.random.split(jax.random.key(seed), 6)
    return {
        "memory": draw_memory(jax.random.fold_in(streams_of[5], 71), 0),
        "decoder_rows": draw_decoder_rows(jax.random.fold_in(streams_of[5], 71), 0),
        "gains": jnp.clip(1.0 + 0.1 * jax.random.normal(streams_of[2], (2, D), jnp.float32), 0.5, 1.5).astype(jnp.bfloat16),
        "weights": draw_weights(jax.random.fold_in(streams_of[5], 71), 0),
        "lengths": draw_lengths(jax.random.fold_in(streams_of[5], 71), 0),
    }


norm_eps = 1e-06
masked_score = -1e+30

def rms_rows(rows, gain):
    wide = rows.astype(jnp.float32)
    inverse = lax.rsqrt(lax.optimization_barrier(jnp.mean(wide * wide, axis=-1, keepdims=True)) + norm_eps)
    return (wide * inverse * gain.astype(jnp.float32)[None, :]).astype(jnp.bfloat16)

def one_head(head_inputs):
    query_head, key_head, value_head, valid_keys = head_inputs
    scores = jnp.dot(query_head, key_head.T, preferred_element_type=jnp.float32)
    masked = jnp.where(valid_keys[None, :], scores, masked_score)
    row_max = lax.optimization_barrier(jnp.max(masked, axis=1, keepdims=True))
    exp_scores = jnp.where(valid_keys[None, :], jnp.exp(masked - row_max), 0.0)
    row_total = lax.optimization_barrier(jnp.sum(exp_scores, axis=1, keepdims=True))
    summed = jnp.dot(exp_scores.astype(jnp.bfloat16), value_head, preferred_element_type=jnp.float32)
    return (summed / row_total).astype(jnp.bfloat16)

def one_doc(doc_inputs):
    query_doc, key_doc, value_doc, length = doc_inputs
    valid_keys = jnp.arange(MEM, dtype=jnp.int32) < length
    query_heads = jnp.transpose(query_doc.reshape(LEN, HEADS, DKV), (1, 0, 2))
    key_heads = jnp.transpose(key_doc.reshape(MEM, HEADS, DKV), (1, 0, 2))
    value_heads = jnp.transpose(value_doc.reshape(MEM, HEADS, DKV), (1, 0, 2))
    repeated = jnp.broadcast_to(valid_keys[None, :], (HEADS, MEM))
    context = lax.map(one_head, (query_heads, key_heads, value_heads, repeated))
    return jnp.transpose(context, (1, 0, 2)).reshape(LEN, HD)

def reference(memory, decoder_rows, gains, weights, lengths):
    memory_rows = rms_rows(memory.reshape(DOCS * MEM, D), gains[0])
    target_rows = rms_rows(decoder_rows.reshape(DOCS * LEN, D), gains[1])
    keys = jnp.dot(memory_rows, weights[0, 0], preferred_element_type=jnp.float32).astype(jnp.bfloat16)
    values = jnp.dot(memory_rows, weights[0, 1], preferred_element_type=jnp.float32).astype(jnp.bfloat16)
    queries = jnp.dot(target_rows, weights[1, 0], preferred_element_type=jnp.float32).astype(jnp.bfloat16)
    context = lax.map(one_doc, (queries.reshape(DOCS, LEN, HD), keys.reshape(DOCS, MEM, HD), values.reshape(DOCS, MEM, HD), lengths.astype(jnp.int32)))
    update = lax.dot_general(context.reshape(DOCS * LEN, HD), weights[1, 1], (((1,), (1,)), ((), ())), preferred_element_type=jnp.float32)
    decoder_out = (decoder_rows.reshape(DOCS * LEN, D).astype(jnp.float32) + update).astype(jnp.bfloat16)
    return decoder_out.reshape(DOCS, LEN, D)
```

```python
import functools

import jax
import jax.numpy as jnp
from jax import lax
from jax.experimental import pallas as pl
from jax.experimental.pallas import tpu as pltpu
from jax.sharding import PartitionSpec as P

DKV = 64
norm_eps = 1e-06
masked_score = -1e30
PAIR = 2 * DKV
STEP_PAIRS = 2
STAT_ROWS = 16
VMEM = pl.BlockSpec(memory_space=pltpu.VMEM)
SMEM = pl.BlockSpec(memory_space=pltpu.SMEM)
ANY = pl.BlockSpec(memory_space=pl.ANY)
f32 = jnp.float32
bf16 = jnp.bfloat16


def params():
    return pltpu.CompilerParams(vmem_limit_bytes=48 * 1024 * 1024)


def normed_parts(parts, gain_ref, info):
    wide = [part[...].astype(f32) for part in parts]
    squares = sum(jnp.sum(w * w, axis=1, keepdims=True) for w in wide)
    features = sum(w.shape[1] for w in wide)
    inverse = lax.rsqrt(squares / features + norm_eps)
    return [
        (w * inverse * gain_ref[pl.ds(info[2 + k], 1), :]).astype(bf16)
        for k, w in enumerate(wide)
    ]


def query_kernel(info, x0, x1, x2, x3, gain, weights, out, res, wbuf, sem):
    parts = (x0, x1, x2, x3)
    width = x0.shape[1]

    def copy(k):
        return pltpu.make_async_copy(
            weights.at[0, 0, pl.ds(info[2 + k] * width, width), :], wbuf.at[k], sem.at[k]
        )

    @pl.when(info[0] == 1)
    def _():
        for k in range(4):
            copy(k).start()
        rows = normed_parts(parts, gain, info)
        half = width // 2
        offset = pl.multiple_of(info[6] * half, half)
        for k in range(4):
            for side in range(2):

                @pl.when(info[7 + side] == k)
                def _():
                    res[:, side * half : (side + 1) * half] = parts[k][:, pl.ds(offset, half)]

        total = None
        for k in range(4):
            copy(k).wait()
            term = jnp.dot(rows[k], wbuf[k], preferred_element_type=f32)
            total = term if total is None else total + term
        out[...] = total.astype(bf16)


def memory_kernel(info, x0, x1, x2, x3, gain, weights, key_out, value_out, wbuf, acc, sem):
    parts = (x0, x1, x2, x3)
    width = x0.shape[1]

    def copy(k, which):
        return pltpu.make_async_copy(
            weights.at[0, which, pl.ds(info[2 + k] * width, width), :],
            wbuf.at[k, which],
            sem.at[k, which],
        )

    @pl.when(info[0] == 0)
    def _():
        for k in range(4):
            for which in range(2):
                copy(k, which).start()
        rows = normed_parts(parts, gain, info)
        for k in range(4):
            for which in range(2):
                copy(k, which).wait()
                term = jnp.dot(rows[k], wbuf[k, which], preferred_element_type=f32)
                if k == 0:
                    acc[which] = term
                elif k < 3:
                    acc[which] += term
                else:
                    out = key_out if which == 0 else value_out
                    out[...] = (acc[which] + term).astype(bf16)


def attention_kernel(count, docs, info, lengths, *refs):
    q_refs, k_refs, v_refs = (
        refs[:count],
        refs[count : count + docs],
        refs[count + docs : count + 2 * docs],
    )
    out = refs[-1]
    span = k_refs[0].shape[0]
    pos = q_refs[0].shape[0] // docs
    group = min(4, count)
    lanes = group * pos

    @pl.when(info[0] == 0)
    def _():
        first = info[1] * span
        lane = lax.broadcasted_iota(jnp.int32, (1, PAIR), 1)
        low = lane < DKV
        positions = first + lax.broadcasted_iota(jnp.int32, (span, 1), 0)
        for base in range(0, count, group):
            stats = [[] for _ in range(group)]
            for pair in range(STEP_PAIRS):
                cols = slice(pair * PAIR, (pair + 1) * PAIR)
                contexts, lses = [], []
                for b in range(docs):
                    rows = jnp.concatenate(
                        [q_refs[base + j][b * pos : (b + 1) * pos, cols] for j in range(group)], axis=0
                    )
                    zero = jnp.zeros_like(rows)
                    both = jnp.concatenate(
                        [jnp.where(low, rows, zero), jnp.where(low, zero, rows)], axis=0
                    )
                    scores = lax.dot_general(
                        k_refs[b][:, cols], both, (((1,), (1,)), ((), ())), preferred_element_type=f32
                    )
                    masked = jnp.where(positions < lengths[b], scores, masked_score)
                    top = jnp.max(masked, axis=0, keepdims=True)
                    probs = jnp.exp(masked - top)
                    total = jnp.sum(probs, axis=0, keepdims=True)
                    summed = lax.dot_general(
                        v_refs[b][:, cols],
                        probs.astype(bf16),
                        (((0,), (0,)), ((), ())),
                        preferred_element_type=f32,
                    )
                    scaled = summed / total
                    lse = jnp.where(first < lengths[b], top + jnp.log(total), masked_score)
                    contexts.append(
                        jnp.concatenate([scaled[:DKV, :lanes], scaled[DKV:, lanes:]], axis=0)
                    )
                    lses.append(lse)
                for j in range(group):
                    block = slice((j // 2) * PAIR, (j // 2 + 1) * PAIR)

                    def placed(first_doc, second_doc):
                        if j % 2 == 0:
                            return jnp.where(low, first_doc, pltpu.roll(second_doc, DKV, 1))
                        return jnp.where(low, pltpu.roll(first_doc, DKV, 1), second_doc)

                    out[base + j, 0, pair * PAIR : (pair + 1) * PAIR, :] = placed(
                        contexts[0][:, block], contexts[1][:, block]
                    ).astype(bf16)
                    for head in range(2):
                        shifted = slice(block.start + head * lanes, block.stop + head * lanes)
                        stats[j].append(
                            placed(
                                jnp.broadcast_to(lses[0][:, shifted], (8, PAIR)),
                                jnp.broadcast_to(lses[1][:, shifted], (8, PAIR)),
                            )[:1]
                        )
            for j in range(group):
                lse = jnp.concatenate(stats[j], axis=0)
                high = lse.astype(bf16).astype(f32)
                middle = (lse - high).astype(bf16).astype(f32)
                rest = lse - high - middle
                packed = jnp.concatenate([high, middle, rest, jnp.zeros_like(rest)], axis=0)
                out[base + j, 0, STEP_PAIRS * PAIR :, :] = packed.astype(bf16)


def combine_kernel(info, *refs):
    sources, out = (refs[:-1], refs[-1])
    slabs = out.shape[0] // (STEP_PAIRS * PAIR)
    heads = 2 * STEP_PAIRS

    @pl.when(info[0] == 0)
    def _():
        for slab in range(slabs):
            lses = []
            for source in sources:
                packed = source[slab, STEP_PAIRS * PAIR :, :].astype(f32)
                lses.append(
                    packed[:heads] + packed[heads : 2 * heads] + packed[2 * heads : 3 * heads]
                )
            top = functools.reduce(jnp.maximum, lses)
            shares = [jnp.exp(lse - top) for lse in lses]
            inverse = 1.0 / sum(shares)
            shares = [share * inverse for share in shares]
            for head in range(heads):
                rows = slice(head * DKV, (head + 1) * DKV)
                context = sum(
                    source[slab, rows, :].astype(f32) * share[head : head + 1]
                    for source, share in zip(sources, shares)
                )
                start = slab * STEP_PAIRS * PAIR + head * DKV
                out[start : start + DKV, :] = context.astype(bf16)


def project_kernel(mask, info, context, weights, out, wbuf, sem):
    block = out.shape[0] // 4
    targets = [(mask ^ 2, 0), (mask ^ 2, 4), (mask, 0), (mask, 4)]

    def copy(i):
        k, add = targets[i]
        return pltpu.make_async_copy(
            weights.at[0, 1, pl.ds((info[2 + k] + add) * block, block), :], wbuf.at[i], sem.at[i]
        )

    @pl.when(info[0] == 1)
    def _():
        for i in range(4):
            copy(i).start()
        for i in range(4):
            copy(i).wait()
            out[i * block : (i + 1) * block, :] = jnp.dot(
                wbuf[i], context[...], preferred_element_type=f32
            ).astype(bf16)


def add_kernel(info, mine, other, out):
    @pl.when(info[0] == 1)
    def _():
        rows = out.shape[0]
        out[...] = (mine[:rows].astype(f32) + other[:rows].astype(f32)).astype(bf16)


def final_kernel(info, mine, sibling, across, res, out):
    @pl.when(info[0] == 1)
    def _():
        half = out.shape[2]
        rows = 2 * half
        for side in range(2):
            part = slice(rows + side * half, rows + (side + 1) * half)
            update = (
                mine[part].astype(f32)
                + sibling[part].astype(f32)
                + across[side * half : (side + 1) * half].astype(f32)
            )
            out[side] = (res[:, side * half : (side + 1) * half].astype(f32) + update.T).astype(bf16)


def call(kernel, out_shapes, args, specs, scratch=(), out_specs=None, flops=0, moved=0, **more):
    return pl.pallas_call(
        kernel,
        out_shape=out_shapes,
        in_specs=specs,
        out_specs=out_specs if out_specs is not None else jax.tree.map(lambda _: VMEM, out_shapes),
        scratch_shapes=list(scratch),
        compiler_params=params(),
        cost_estimate=pl.CostEstimate(flops=flops, bytes_accessed=moved, transcendentals=0),
        **more,
    )(*args)


def on_device(memory, decoder_rows, gains, weights, lengths):
    segment = lax.axis_index("segment")
    seq = lax.axis_index("seq")
    m = lax.axis_index("mp")
    count = lax.axis_size("seq")
    docs, span, width = memory.shape
    pos = decoder_rows.shape[1]
    rows = docs * pos
    head_width = weights.shape[3]

    info = jnp.stack(
        [segment, seq, m, m ^ 1, m ^ 2, m ^ 3, m % 2, m ^ (m // 2), m ^ (2 + m // 2)]
    ).astype(jnp.int32)
    gain = gains.astype(f32).reshape(4, width)
    lengths = lengths.astype(jnp.int32)

    def in_section(array, section, mask):
        pairs = [(section * 4 + i, section * 4 + (i ^ mask)) for i in range(4)]
        return lax.ppermute(array, ("segment", "mp"), pairs)

    def along_seq(array, section, by):
        pairs = [(section * count + i, section * count + (i + by) % count) for i in range(count)]
        return lax.ppermute(array, ("segment", "seq"), pairs)

    dec = decoder_rows.reshape(rows, width)
    dec_y = in_section(dec, 1, 2)
    dec_c = in_section(dec, 1, 1)
    mem_docs = [memory[b] for b in range(docs)]
    mem_c = [in_section(mem_docs[b], 0, 1) for b in range(docs)]
    mem_y = [in_section(mem_docs[b], 0, 2) for b in range(docs)]
    dec_yc = in_section(dec_y, 1, 1)

    queries, residual = call(
        query_kernel,
        (
            jax.ShapeDtypeStruct((rows, head_width), bf16),
            jax.ShapeDtypeStruct((rows, width), bf16),
        ),
        (info, dec, dec_c, dec_y, dec_yc, gain, weights),
        [SMEM, VMEM, VMEM, VMEM, VMEM, VMEM, ANY],
        [pltpu.VMEM((4, width, head_width), bf16), pltpu.SemaphoreType.DMA((4,))],
        flops=2 * rows * 4 * width * head_width,
        moved=8 * width * head_width,
    )
    pairs = [(1, 0)]
    q_pieces = [lax.ppermute(queries, "segment", pairs)]
    for by in range(1, count):
        q_pieces.append(along_seq(q_pieces[0], 0, by))

    keys, values = [], []
    for b in range(docs):
        mem_yc = in_section(mem_y[b], 0, 1)
        key, value = call(
            memory_kernel,
            (
                jax.ShapeDtypeStruct((span, head_width), bf16),
                jax.ShapeDtypeStruct((span, head_width), bf16),
            ),
            (info, mem_docs[b], mem_c[b], mem_y[b], mem_yc, gain, weights),
            [SMEM, VMEM, VMEM, VMEM, VMEM, VMEM, ANY],
            [
                pltpu.VMEM((4, 2, width, head_width), bf16),
                pltpu.VMEM((2, span, head_width), f32),
                pltpu.SemaphoreType.DMA((4, 2)),
            ],
            flops=4 * span * 4 * width * head_width,
            moved=16 * width * head_width,
        )
        keys.append(key)
        values.append(value)

    step_width = STEP_PAIRS * PAIR
    steps = head_width // step_width
    slab = step_width + STAT_ROWS
    column = lambda height: pl.BlockSpec((height, step_width), lambda i: (0, i))
    partial = call(
        functools.partial(attention_kernel, count, docs),
        jax.ShapeDtypeStruct((count, steps, slab, rows), bf16),
        (info, lengths, *q_pieces, *keys, *values),
        [SMEM, SMEM] + [column(rows)] * count + [column(span)] * (2 * docs),
        out_specs=pl.BlockSpec((count, 1, slab, rows), lambda i: (0, i, 0, 0)),
        grid=(steps,),
        flops=8 * rows * count * span * head_width,
        moved=4 * rows * count * head_width,
    )
    sources = [partial[0]] + [along_seq(partial[by], 0, -by) for by in range(1, count)]
    context = call(
        combine_kernel,
        jax.ShapeDtypeStruct((head_width, rows), bf16),
        (info, *sources),
        [SMEM] + [VMEM] * count,
        flops=8 * rows * count * head_width,
        moved=2 * rows * count * head_width,
    )
    context = lax.ppermute(context, "segment", [(0, 1)])

    block = 4 * width // 8

    def project(mask):
        return call(
            functools.partial(project_kernel, mask),
            jax.ShapeDtypeStruct((4 * block, rows), bf16),
            (info, context, weights),
            [SMEM, VMEM, ANY],
            [pltpu.VMEM((4, block, head_width), bf16), pltpu.SemaphoreType.DMA((4,))],
            flops=2 * rows * 4 * block * head_width,
            moved=8 * block * head_width,
        )

    for_sibling = project(1)
    sibling = in_section(for_sibling, 1, 1)
    mine = project(0)
    for_across = call(
        add_kernel,
        jax.ShapeDtypeStruct((2 * block, rows), bf16),
        (info, mine, sibling),
        [SMEM, VMEM, VMEM],
        moved=12 * block * rows,
    )
    across = in_section(for_across, 1, 2)
    done = call(
        final_kernel,
        jax.ShapeDtypeStruct((2, rows, block), bf16),
        (info, mine, sibling, across, residual),
        [SMEM, VMEM, VMEM, VMEM, VMEM],
        moved=20 * block * rows,
    )
    received = lax.ppermute(done[0], "segment", pairs)
    decoder_out = jnp.where(segment == 0, received, done[1])
    return decoder_out.reshape(docs, pos, block)


def solution(mesh):
    in_specs = (
        P(None, "seq", "mp"),
        P(None, "seq", "mp"),
        P("segment", None),
        P("segment", None, None, "mp"),
        P(),
    )
    out_specs = P(None, "seq", ("segment", "mp"))
    return jax.shard_map(
        on_device, mesh=mesh, in_specs=in_specs, out_specs=out_specs, check_vma=False
    )
```

```python
import functools

import jax
import jax.numpy as jnp
from jax import lax
from jax.experimental import pallas as pl
from jax.experimental.pallas import tpu as pltpu
from jax.sharding import PartitionSpec as P

DKV = 64
norm_eps = 1e-06
masked_score = -1e30
PAIR = 2 * DKV
LANES = 128
STAT_LANES = 128
CHUNKS = 8
IN_FLIGHT = 99
VMEM = pl.BlockSpec(memory_space=pltpu.VMEM)
SMEM = pl.BlockSpec(memory_space=pltpu.SMEM)
ANY = pl.BlockSpec(memory_space=pl.ANY)
f32 = jnp.float32
bf16 = jnp.bfloat16


def params():
    return pltpu.CompilerParams(vmem_limit_bytes=44 * 1024 * 1024)


def position():
    m = lax.axis_index("mp")
    return (
        lax.axis_index("segment"),
        lax.axis_index("seq"),
        m,
        m ^ 1,
        m ^ 2,
        m ^ 3,
        m & 1,
        m ^ (m >> 1),
        m ^ (2 + (m >> 1)),
    )


def squares(parts):
    return sum(jnp.sum(jnp.square(part.astype(f32)), axis=1, keepdims=True) for part in parts)


def gained(rows, inverse, gains, block):
    width = rows.shape[1]
    gain = gains[:, pl.ds(pl.multiple_of(block * width, width), width)].astype(f32)
    return (rows.astype(f32) * inverse * gain).astype(bf16)


class WeightStream:
    def __init__(self, weights, order, width, wbuf, sem):
        height = wbuf.shape[1]
        self.copies = [
            pltpu.make_async_copy(
                weights.at[0, which, pl.ds(block * width + start, height), :],
                wbuf.at[i],
                sem.at[i],
            )
            for i, (which, block, start) in enumerate(
                (which, block, start)
                for which, block in order
                for start in range(0, width, height)
            )
        ]
        self.wbuf = wbuf
        self.started = self.used = 0
        for _ in range(IN_FLIGHT):
            self.start()

    def start(self):
        if self.started < len(self.copies):
            self.copies[self.started].start()
            self.started += 1

    def product(self, rows):
        height = self.wbuf.shape[1]
        total = None
        for start in range(0, rows.shape[1], height):
            self.copies[self.used].wait()
            self.start()
            term = jnp.dot(
                rows[:, start : start + height], self.wbuf[self.used], preferred_element_type=f32
            )
            total = term if total is None else total + term
            self.used += 1
        return total


def normed_rows(parts, gains, blocks):
    inverse = lax.rsqrt(squares(parts) / gains.shape[1] + norm_eps)
    return [gained(part, inverse, gains, block) for part, block in zip(parts, blocks)]


def streamed_product(rows, stream):
    return sum(stream.product(part) for part in rows)


def near_copy_kernel(dec, gains, dec_out, gains_out):
    dec_out[...] = dec[...]
    gains_out[...] = gains[...]


def query_kernel(x0, x1, x2, x3, gains, weights, first_out, second_out, res, wbuf, sem):
    info = position()
    blocks = info[2:6]
    rows_each = first_out.shape[0]

    @pl.when(info[0] == 1)
    def _():
        stream = WeightStream(weights, [(0, block) for block in blocks], x0.shape[1], wbuf, sem)
        half = res.shape[1] // 2
        offset = pl.multiple_of(info[6] * half, half)
        for k, part in enumerate((x0, x1, x2, x3)):
            for side in range(2):

                @pl.when(info[7 + side] == k)
                def _():
                    res[:, side * half : (side + 1) * half] = part[:, pl.ds(offset, half)]

        parts = (x0[...], x1[...], x2[...], x3[...])
        total = streamed_product(normed_rows(parts, gains, blocks), stream)
        first_out[...] = total[:rows_each].astype(bf16)
        second_out[...] = total[rows_each:].astype(bf16)


def memory_kernel(doc, matrices, x0, x1, x2, x3, gains, weights, out, wbuf, sem):
    info = position()
    blocks = info[2:6]
    span = x2.shape[0]
    here = slice(doc * span, (doc + 1) * span)

    @pl.when(info[0] == 0)
    def _():
        order = [(which, block) for which in matrices for block in blocks]
        stream = WeightStream(weights, order, x2.shape[1], wbuf, sem)
        parts = (x0[here], x1[here], x2[...], x3[...])
        rows = normed_rows(parts, gains, blocks)
        for i in range(len(matrices)):
            out[i] = streamed_product(rows, stream).astype(bf16)


def attention_kernel(count, lengths, *refs):
    info = position()
    for side in range(2):

        @pl.when(info[0] == side)
        def _():
            attend(
                lengths[1 - side],
                info[1],
                refs[:count],
                refs[count + side],
                refs[count + 2 :],
            )


def attend(length, seq, q_refs, key_values, outs):
    count = len(q_refs)
    keys, values = (key_values.at[0], key_values.at[1])
    span = keys.shape[0]
    pos, head_width = q_refs[0].shape
    group = min(4, count)
    rows_here = group * pos
    first = seq * span
    lane = lax.broadcasted_iota(jnp.int32, (1, PAIR), 1)
    low = lane < DKV
    valid = first + lax.broadcasted_iota(jnp.int32, (1, span), 1) < length
    for base in range(0, count, group):
        stats = jnp.zeros((rows_here, STAT_LANES), f32)
        for pair in range(head_width // PAIR):
            cols = slice(pair * PAIR, (pair + 1) * PAIR)
            rows = jnp.concatenate([q_refs[base + j][:, cols] for j in range(group)], axis=0)
            zero = jnp.zeros_like(rows)
            both = jnp.concatenate(
                [jnp.where(low, rows, zero), jnp.where(low, zero, rows)], axis=0
            )
            scores = lax.dot_general(
                both, keys[:, cols], (((1,), (1,)), ((), ())), preferred_element_type=f32
            )
            masked = jnp.where(valid, scores, masked_score)
            top = jnp.max(masked, axis=1, keepdims=True)
            probs = jnp.exp(masked - top)
            total = jnp.sum(probs, axis=1, keepdims=True)
            summed = jnp.dot(probs.astype(bf16), values[:, cols], preferred_element_type=f32)
            scaled = summed * (1.0 / total)
            lse = jnp.where(first < length, top + jnp.log(total), masked_score)
            context = jnp.where(low, scaled[:rows_here], scaled[rows_here:]).astype(bf16)
            for j in range(group):
                outs[base + j][:, cols] = context[j * pos : (j + 1) * pos]
            stats = jnp.where(lane == 2 * pair, lse[:rows_here], stats)
            stats = jnp.where(lane == 2 * pair + 1, lse[rows_here:], stats)
        heads = head_width // DKV
        high = stats.astype(bf16).astype(f32)
        middle = (stats - high).astype(bf16).astype(f32)
        rest = stats - high - middle
        packed = high + pltpu.roll(middle, heads, 1) + pltpu.roll(rest, 2 * heads, 1)
        for j in range(group):
            outs[base + j][:, head_width:] = packed[j * pos : (j + 1) * pos].astype(bf16)


def combine_kernel(*refs):
    sources, out = (refs[:-1], refs[-1])
    head_width = out.shape[1]
    heads = head_width // DKV
    low = lax.broadcasted_iota(jnp.int32, (1, PAIR), 1) < DKV
    lses = []
    for source in sources:
        packed = source[:, head_width:].astype(f32)
        lses.append(
            packed
            + pltpu.roll(packed, STAT_LANES - heads, 1)
            + pltpu.roll(packed, STAT_LANES - 2 * heads, 1)
        )
    top = functools.reduce(jnp.maximum, lses)
    shares = [jnp.exp(lse - top) for lse in lses]
    inverse = 1.0 / sum(shares)
    shares = [share * inverse for share in shares]
    for pair in range(heads // 2):
        cols = slice(pair * PAIR, (pair + 1) * PAIR)
        context = sum(
            source[:, cols].astype(f32)
            * jnp.where(low, share[:, 2 * pair : 2 * pair + 1], share[:, 2 * pair + 1 : 2 * pair + 2])
            for source, share in zip(sources, shares)
        )
        out[:, cols] = context.astype(bf16)


def load_kernel(weights, context, out, sem):
    info = position()
    @pl.when(info[0] == 1)
    def _():
        height = out.shape[0] // 8
        copies = [
            pltpu.make_async_copy(
                weights.at[0, 1, pl.ds(i * height, height), :],
                out.at[pl.ds(i * height, height), :],
                sem.at[i],
            )
            for i in range(8)
        ]
        for copy in copies:
            copy.start()
        for copy in copies:
            copy.wait()


def project_kernel(mask, first_context, second_context, weights, out):
    info = position()
    block = out.shape[0] // 4
    targets = [(mask ^ 2, 0), (mask ^ 2, 4), (mask, 0), (mask, 4)]

    @pl.when(info[0] == 1)
    def _():
        context = jnp.concatenate([first_context[...], second_context[...]], axis=0)
        for i, (k, add) in enumerate(targets):
            start = pl.multiple_of((info[2 + k] + add) * block, block)
            out[i * block : (i + 1) * block, :] = lax.dot_general(
                weights[pl.ds(start, block), :],
                context,
                (((1,), (1,)), ((), ())),
                preferred_element_type=f32,
            ).astype(bf16)


def add_kernel(mine, other, out):
    info = position()
    @pl.when(info[0] == 1)
    def _():
        rows = out.shape[0]
        out[...] = (mine[:rows].astype(f32) + other[:rows].astype(f32)).astype(bf16)


def final_kernel(mine, sibling, across, res, *outs):
    info = position()
    @pl.when(info[0] == 1)
    def _():
        half = outs[0].shape[1]
        rows = 2 * half
        for side, out in enumerate(outs):
            part = slice(rows + side * half, rows + (side + 1) * half)
            update = (
                mine[part].astype(f32)
                + sibling[part].astype(f32)
                + across[side * half : (side + 1) * half].astype(f32)
            )
            out[...] = (res[:, side * half : (side + 1) * half].astype(f32) + update.T).astype(bf16)


def call(kernel, out_shapes, args, specs, scratch=(), out_specs=None, flops=1, **more):
    return pl.pallas_call(
        kernel,
        out_shape=out_shapes,
        in_specs=specs,
        out_specs=out_specs if out_specs is not None else jax.tree.map(lambda _: VMEM, out_shapes),
        scratch_shapes=list(scratch),
        compiler_params=params(),
        cost_estimate=pl.CostEstimate(flops=flops, bytes_accessed=1, transcendentals=0),
        **more,
    )(*args)


def on_device(memory, decoder_rows, gains, weights, lengths):
    segment = lax.axis_index("segment")
    seq = lax.axis_index("seq")
    m = lax.axis_index("mp")
    count = lax.axis_size("seq")
    docs, span, width = memory.shape
    pos = decoder_rows.shape[1]
    rows = docs * pos
    head_width = weights.shape[3]

    lengths = lengths.astype(jnp.int32)
    shape = lambda *dims: jax.ShapeDtypeStruct(dims, bf16)
    after = lax.optimization_barrier

    def in_section(array, section, mask):
        pairs = [(section * 4 + i, section * 4 + (i ^ mask)) for i in range(4)]
        return lax.ppermute(array, ("segment", "mp"), pairs)

    def along_seq(array, by):
        return lax.ppermute(array, "seq", [(i, (i + by) % count) for i in range(count)])

    def to_encoder(array):
        return lax.ppermute(array, "segment", [(1, 0)])

    def to_decoder(array):
        return lax.ppermute(array, "segment", [(0, 1)])

    dec = decoder_rows.reshape(rows, width)
    dec_y = in_section(dec, 1, 2)
    dec_c = in_section(dec, 1, 1)
    extra = span * 64 // 256
    first_rows, memory = after((memory[0], memory))
    mem = memory.reshape(docs * span, width)
    mem_y = [in_section(first_rows, 0, 2), in_section(mem[span - extra :], 0, 2)]
    mem_c = in_section(mem, 0, 1)

    def weight_scratch(matrices):
        chunks = matrices * CHUNKS
        return [
            pltpu.VMEM((chunks, 4 * width // CHUNKS, head_width), bf16),
            pltpu.SemaphoreType.DMA((chunks,)),
        ]

    dec_here, gains = call(
        near_copy_kernel, (shape(rows, width), shape(*gains.shape)), (dec, gains), [VMEM] * 2
    )
    dec_y, _ = after((dec_y, gains))
    dec_yc = in_section(dec_y, 1, 1)
    first_queries, second_queries, residual = call(
        query_kernel,
        (shape(pos, head_width), shape(pos, head_width), shape(rows, width)),
        (dec_here, dec_c, dec_y, dec_yc, gains, weights),
        [VMEM] * 5 + [ANY],
        weight_scratch(1),
    )
    q_received = to_encoder(second_queries)

    def project_memory(doc, matrices, far, far_c, cost):
        return call(
            functools.partial(memory_kernel, doc, matrices),
            shape(len(matrices), span, head_width),
            (mem, mem_c, far, far_c, gains, weights),
            [VMEM] * 5 + [ANY],
            weight_scratch(len(matrices)),
            flops=int(cost),
        )

    far, _ = after((mem_y[0], second_queries))
    far_c = in_section(far, 0, 1)
    made = project_memory(0, (0, 1), far, far_c, 1)
    first_memory = to_decoder(made)
    q_received, _ = after((q_received, made))
    far, _ = after((mem_y[1], q_received))
    far = far[extra:]
    second_memory = project_memory(1, (0, 1), far, in_section(far, 0, 1), 4.8e9)

    encoding = segment == 0
    q_pieces = [jnp.where(encoding, q_received, first_queries)]
    for by in range(1, count):
        q_pieces.append(along_seq(q_pieces[0], by))

    partial = call(
        functools.partial(attention_kernel, count),
        (shape(pos, head_width + STAT_LANES),) * count,
        (lengths, *q_pieces, second_memory, first_memory),
        [SMEM] + [VMEM] * (count + 2),
    )
    sources = [partial[0]] + [along_seq(partial[by], -by) for by in range(1, count)]
    context = call(
        combine_kernel,
        shape(pos, head_width),
        tuple(sources),
        [VMEM] * count,
    )
    second_context = to_decoder(context)

    last_weights = call(
        load_kernel,
        shape(4 * width, head_width),
        (weights, context),
        [ANY, ANY],
        [pltpu.SemaphoreType.DMA((8,))],
    )
    block = 4 * width // 8

    def project(mask):
        return call(
            functools.partial(project_kernel, mask),
            shape(4 * block, rows),
            (context, second_context, last_weights),
            [VMEM, VMEM, VMEM],
        )

    for_sibling = project(1)
    sibling = in_section(for_sibling, 1, 1)
    mine = project(0)
    for_across = call(
        add_kernel,
        shape(2 * block, rows),
        (mine, sibling),
        [VMEM, VMEM],
    )
    across = in_section(for_across, 1, 2)
    for_encoder, own = call(
        final_kernel,
        (shape(rows, block), shape(rows, block)),
        (mine, sibling, across, residual),
        [VMEM, VMEM, VMEM, VMEM],
    )
    received = to_encoder(for_encoder)
    decoder_out = jnp.where(encoding, received, own)
    return decoder_out.reshape(docs, pos, block)


def solution(mesh):
    in_specs = (
        P(None, "seq", "mp"),
        P(None, "seq", "mp"),
        P("segment", None),
        P("segment", None, None, "mp"),
        P(),
    )
    out_specs = P(None, "seq", ("segment", "mp"))
    return jax.shard_map(
        on_device, mesh=mesh, in_specs=in_specs, out_specs=out_specs, check_vma=False
    )
```

```python
import functools

import jax
import jax.numpy as jnp
from jax import lax
from jax.experimental import pallas as pl
from jax.experimental.pallas import tpu as pltpu
from jax.sharding import PartitionSpec as P

DKV = 64
norm_eps = 1e-06
masked_score = -1e30
PAIR = 2 * DKV
LANES = 128
STAT_LANES = 128
CHUNKS = 8
IN_FLIGHT = 99
VMEM = pl.BlockSpec(memory_space=pltpu.VMEM)
SMEM = pl.BlockSpec(memory_space=pltpu.SMEM)
ANY = pl.BlockSpec(memory_space=pl.ANY)
f32 = jnp.float32
bf16 = jnp.bfloat16


def params():
    return pltpu.CompilerParams(vmem_limit_bytes=40 * 1024 * 1024)


def position():
    m = lax.axis_index("mp")
    return (
        lax.axis_index("segment"),
        lax.axis_index("seq"),
        m,
        m ^ 1,
        m ^ 2,
        m ^ 3,
        m & 1,
        m ^ (m >> 1),
        m ^ (2 + (m >> 1)),
    )


def squares(parts):
    return sum(jnp.sum(jnp.square(part.astype(f32)), axis=1, keepdims=True) for part in parts)


def gained(rows, inverse, gains, block):
    width = rows.shape[1]
    gain = gains[:, pl.ds(pl.multiple_of(block * width, width), width)].astype(f32)
    return (rows.astype(f32) * inverse * gain).astype(bf16)


class WeightStream:
    def __init__(self, weights, order, width, wbuf, sem):
        height = wbuf.shape[1]
        self.copies = [
            pltpu.make_async_copy(
                weights.at[0, which, pl.ds(block * width + start, height), :],
                wbuf.at[i],
                sem.at[i],
            )
            for i, (which, block, start) in enumerate(
                (which, block, start)
                for which, block in order
                for start in range(0, width, height)
            )
        ]
        self.wbuf = wbuf
        self.started = self.used = 0
        for _ in range(IN_FLIGHT):
            self.start()

    def start(self):
        if self.started < len(self.copies):
            self.copies[self.started].start()
            self.started += 1

    def product(self, rows):
        height = self.wbuf.shape[1]
        total = None
        for start in range(0, rows.shape[1], height):
            self.copies[self.used].wait()
            self.start()
            term = jnp.dot(
                rows[:, start : start + height], self.wbuf[self.used], preferred_element_type=f32
            )
            total = term if total is None else total + term
            self.used += 1
        return total


def normed_rows(parts, gains, blocks):
    inverse = lax.rsqrt(squares(parts) / gains.shape[1] + norm_eps)
    return [gained(part, inverse, gains, block) for part, block in zip(parts, blocks)]


def streamed_product(rows, stream):
    return sum(stream.product(part) for part in rows)


def near_copy_kernel(dec, gains, dec_out, gains_out):
    dec_out[...] = dec[...]
    gains_out[...] = gains[...]


def query_kernel(x0, x1, x2, x3, gains, weights, first_out, second_out, res1, wbuf, sem):
    info = position()
    blocks = info[2:6]
    rows_each = first_out.shape[0]

    @pl.when(info[0] == 1)
    def _():
        stream = WeightStream(weights, [(0, block) for block in blocks], x0.shape[1], wbuf, sem)
        half = res1.shape[1]
        offset = pl.multiple_of(info[6] * half, half)
        for k, part in enumerate((x0, x1, x2, x3)):

            @pl.when(info[7] == k)
            def _():
                for doc in range(part.shape[0] // rows_each):
                    second_out[rows_each:, doc * half : (doc + 1) * half] = part[
                        doc * rows_each : (doc + 1) * rows_each, pl.ds(offset, half)
                    ]

            @pl.when(info[8] == k)
            def _():
                res1[...] = part[:, pl.ds(offset, half)]

        parts = (x0[...], x1[...], x2[...], x3[...])
        total = streamed_product(normed_rows(parts, gains, blocks), stream)
        first_out[...] = total[:rows_each].astype(bf16)
        second_out[:rows_each] = total[rows_each:].astype(bf16)


def memory_kernel(doc, matrices, x0, x1, x2, x3, gains, weights, out, wbuf, sem):
    info = position()
    blocks = info[2:6]
    span = x2.shape[0]
    here = slice(doc * span, (doc + 1) * span)

    @pl.when(info[0] == 0)
    def _():
        order = [(which, block) for which in matrices for block in blocks]
        stream = WeightStream(weights, order, x2.shape[1], wbuf, sem)
        parts = (x0[here], x1[here], x2[...], x3[...])
        rows = normed_rows(parts, gains, blocks)
        for i in range(len(matrices)):
            out[i] = streamed_product(rows, stream).astype(bf16)


def first_memory_kernel(x0, x1, x2, x3, gains, key_weights, weights, out, wbuf, sem):
    info = position()
    blocks = info[2:6]
    span, width = x2.shape

    @pl.when(info[0] == 0)
    def _():
        stream = WeightStream(weights, [(1, block) for block in blocks], width, wbuf, sem)
        rows = normed_rows((x0[:span], x1[:span], x2[...], x3[...]), gains, blocks)
        total = None
        for part, block in zip(rows, blocks):
            matrix = key_weights[pl.ds(pl.multiple_of(block * width, width), width), :]
            term = jnp.dot(part, matrix, preferred_element_type=f32)
            total = term if total is None else total + term
        out[0] = total.astype(bf16)
        out[1] = streamed_product(rows, stream).astype(bf16)


def attention_kernel(count, lengths, *refs):
    info = position()
    for side in range(2):

        @pl.when(info[0] == side)
        def _():
            attend(
                lengths[1 - side],
                info[1],
                refs[:count],
                refs[count + side],
                refs[count + 2 :],
            )


def attend(length, seq, q_refs, key_values, outs):
    count = len(q_refs)
    keys, values = (key_values.at[0], key_values.at[1])
    span = keys.shape[0]
    pos, head_width = q_refs[0].shape
    group = min(4, count)
    rows_here = group * pos
    first = seq * span
    lane = lax.broadcasted_iota(jnp.int32, (1, PAIR), 1)
    low = lane < DKV
    valid = first + lax.broadcasted_iota(jnp.int32, (1, span), 1) < length
    for base in range(0, count, group):
        stats = jnp.zeros((rows_here, STAT_LANES), f32)
        for pair in range(head_width // PAIR):
            cols = slice(pair * PAIR, (pair + 1) * PAIR)
            rows = jnp.concatenate([q_refs[base + j][:, cols] for j in range(group)], axis=0)
            zero = jnp.zeros_like(rows)
            both = jnp.concatenate(
                [jnp.where(low, rows, zero), jnp.where(low, zero, rows)], axis=0
            )
            scores = lax.dot_general(
                both, keys[:, cols], (((1,), (1,)), ((), ())), preferred_element_type=f32
            )
            masked = jnp.where(valid, scores, masked_score)
            top = jnp.max(masked, axis=1, keepdims=True)
            probs = jnp.exp(masked - top)
            total = jnp.sum(probs, axis=1, keepdims=True)
            summed = jnp.dot(probs.astype(bf16), values[:, cols], preferred_element_type=f32)
            scaled = summed * (1.0 / total)
            lse = jnp.where(first < length, top + jnp.log(total), masked_score)
            context = jnp.where(low, scaled[:rows_here], scaled[rows_here:]).astype(bf16)
            for j in range(group):
                outs[base + j][:, cols] = context[j * pos : (j + 1) * pos]
            stats = jnp.where(lane == 2 * pair, lse[:rows_here], stats)
            stats = jnp.where(lane == 2 * pair + 1, lse[rows_here:], stats)
        heads = head_width // DKV
        high = stats.astype(bf16).astype(f32)
        middle = (stats - high).astype(bf16).astype(f32)
        rest = stats - high - middle
        packed = high + pltpu.roll(middle, heads, 1) + pltpu.roll(rest, 2 * heads, 1)
        for j in range(group):
            outs[base + j][:, head_width:] = packed[j * pos : (j + 1) * pos].astype(bf16)


def combine_kernel(*refs):
    sources, out = (refs[:-1], refs[-1])
    head_width = out.shape[1]
    heads = head_width // DKV
    low = lax.broadcasted_iota(jnp.int32, (1, PAIR), 1) < DKV
    lses = []
    for source in sources:
        packed = source[:, head_width:].astype(f32)
        lses.append(
            packed
            + pltpu.roll(packed, STAT_LANES - heads, 1)
            + pltpu.roll(packed, STAT_LANES - 2 * heads, 1)
        )
    top = functools.reduce(jnp.maximum, lses)
    shares = [jnp.exp(lse - top) for lse in lses]
    inverse = 1.0 / sum(shares)
    shares = [share * inverse for share in shares]
    for pair in range(heads // 2):
        cols = slice(pair * PAIR, (pair + 1) * PAIR)
        context = sum(
            source[:, cols].astype(f32)
            * jnp.where(low, share[:, 2 * pair : 2 * pair + 1], share[:, 2 * pair + 1 : 2 * pair + 2])
            for source, share in zip(sources, shares)
        )
        out[:, cols] = context.astype(bf16)


def load_kernel(section, which, weights, before, out, sem):
    info = position()

    @pl.when(info[0] == section)
    def _():
        height = out.shape[0] // 8
        copies = [
            pltpu.make_async_copy(
                weights.at[0, which, pl.ds(i * height, height), :],
                out.at[pl.ds(i * height, height), :],
                sem.at[i],
            )
            for i in range(8)
        ]
        for copy in copies:
            copy.start()
        for copy in copies:
            copy.wait()


def project_kernel(mask, first_context, second_context, weights, out):
    info = position()
    block = out.shape[0] // 4
    targets = [(mask ^ 2, 0), (mask ^ 2, 4), (mask, 0), (mask, 4)]

    @pl.when(info[0] == 1)
    def _():
        context = jnp.concatenate([first_context[...], second_context[...]], axis=0)
        for i, (k, add) in enumerate(targets):
            start = pl.multiple_of((info[2 + k] + add) * block, block)
            out[i * block : (i + 1) * block, :] = lax.dot_general(
                weights[pl.ds(start, block), :],
                context,
                (((1,), (1,)), ((), ())),
                preferred_element_type=f32,
            ).astype(bf16)


def add_kernel(mine, other, *outs):
    info = position()

    @pl.when(info[0] == 1)
    def _():
        rows = outs[0].shape[0]
        for i, out in enumerate(outs):
            part = slice(i * rows, (i + 1) * rows)
            out[...] = (mine[part].astype(f32) + other[part].astype(f32)).astype(bf16)


def final_kernel(mine, sibling, across, residual1, direct, diagonal, residual0, out):
    info = position()
    block = out.shape[1]

    @pl.when(info[0] == 1)
    def _():
        part = slice(3 * block, 4 * block)
        update = mine[part].astype(f32) + sibling[part].astype(f32) + across[...].astype(f32)
        out[...] = (residual1[...].astype(f32) + update.T).astype(bf16)

    @pl.when(info[0] == 0)
    def _():
        update = direct[...].astype(f32) + diagonal[...].astype(f32)
        update = update.T
        pos = residual0.shape[0] // 2
        for doc in range(out.shape[0] // pos):
            here = slice(doc * pos, (doc + 1) * pos)
            residual = residual0[pos:, doc * block : (doc + 1) * block].astype(f32)
            out[here] = (residual + update[here]).astype(bf16)


def call(kernel, out_shapes, args, specs, scratch=(), out_specs=None, flops=1, **more):
    return pl.pallas_call(
        kernel,
        out_shape=out_shapes,
        in_specs=specs,
        out_specs=out_specs if out_specs is not None else jax.tree.map(lambda _: VMEM, out_shapes),
        scratch_shapes=list(scratch),
        compiler_params=params(),
        cost_estimate=pl.CostEstimate(flops=flops, bytes_accessed=1, transcendentals=0),
        **more,
    )(*args)


def on_device(memory, decoder_rows, gains, weights, lengths):
    segment = lax.axis_index("segment")
    seq = lax.axis_index("seq")
    m = lax.axis_index("mp")
    count = lax.axis_size("seq")
    docs, span, width = memory.shape
    pos = decoder_rows.shape[1]
    rows = docs * pos
    head_width = weights.shape[3]

    lengths = lengths.astype(jnp.int32)
    shape = lambda *dims: jax.ShapeDtypeStruct(dims, bf16)
    after = lax.optimization_barrier

    def in_section(array, section, mask):
        pairs = [(section * 4 + i, section * 4 + (i ^ mask)) for i in range(4)]
        return lax.ppermute(array, ("segment", "mp"), pairs)

    def along_seq(array, by):
        return lax.ppermute(array, "seq", [(i, (i + by) % count) for i in range(count)])

    def to_encoder(array):
        return lax.ppermute(array, "segment", [(1, 0)])

    def to_decoder(array):
        return lax.ppermute(array, "segment", [(0, 1)])

    dec = decoder_rows.reshape(rows, width)
    dec_y = in_section(dec, 1, 2)
    dec_c = in_section(dec, 1, 1)
    extra = span * 64 // 256
    first_rows, memory = after((memory[0], memory))
    mem = memory.reshape(docs * span, width)
    mem_y = [in_section(first_rows, 0, 2), in_section(mem[span - extra :], 0, 2)]
    mem_c = in_section(mem, 0, 1)

    def weight_scratch(matrices):
        chunks = matrices * CHUNKS
        return [
            pltpu.VMEM((chunks, 4 * width // CHUNKS, head_width), bf16),
            pltpu.SemaphoreType.DMA((chunks,)),
        ]

    dec_here, gains = call(
        near_copy_kernel, (shape(rows, width), shape(*gains.shape)), (dec, gains), [VMEM] * 2
    )
    dec_y, _ = after((dec_y, gains))
    dec_yc = in_section(dec_y, 1, 1)
    first_queries, for_encoder, residual1 = call(
        query_kernel,
        (shape(pos, head_width), shape(2 * pos, head_width), shape(rows, width // 2)),
        (dec_here, dec_c, dec_y, dec_yc, gains, weights),
        [VMEM] * 5 + [ANY],
        weight_scratch(1),
    )
    from_decoder = to_encoder(for_encoder)

    def project_memory(doc, matrices, far, far_c, cost):
        return call(
            functools.partial(memory_kernel, doc, matrices),
            shape(len(matrices), span, head_width),
            (mem, mem_c, far, far_c, gains, weights),
            [VMEM] * 5 + [ANY],
            weight_scratch(len(matrices)),
            flops=int(cost),
        )

    def load(section, which, before):
        return call(
            functools.partial(load_kernel, section, which),
            shape(4 * width, head_width),
            (weights, before),
            [ANY, ANY],
            [pltpu.SemaphoreType.DMA((8,))],
        )

    key_weights = load(0, 0, for_encoder)
    far, _ = after((mem_y[0], key_weights))
    far_c = in_section(far, 0, 1)
    made = call(
        first_memory_kernel,
        shape(2, span, head_width),
        (mem, mem_c, far, far_c, gains, key_weights, weights),
        [VMEM] * 6 + [ANY],
        weight_scratch(1),
    )
    first_memory = to_decoder(made)
    from_decoder, _ = after((from_decoder, made))
    far, _ = after((mem_y[1], from_decoder))
    far = far[extra:]
    second_memory = project_memory(1, (0, 1), far, in_section(far, 0, 1), 4.8e9)

    encoding = segment == 0
    q_pieces = [jnp.where(encoding, from_decoder[:pos], first_queries)]
    for by in range(1, count):
        q_pieces.append(along_seq(q_pieces[0], by))

    partial = call(
        functools.partial(attention_kernel, count),
        (shape(pos, head_width + STAT_LANES),) * count,
        (lengths, *q_pieces, second_memory, first_memory),
        [SMEM] + [VMEM] * (count + 2),
    )
    sources = [partial[0]] + [along_seq(partial[by], -by) for by in range(1, count)]
    context = call(
        combine_kernel,
        shape(pos, head_width),
        tuple(sources),
        [VMEM] * count,
    )
    second_context = to_decoder(context)

    last_weights = load(1, 1, context)
    block = 4 * width // 8

    def project(mask):
        return call(
            functools.partial(project_kernel, mask),
            shape(4 * block, rows),
            (context, second_context, last_weights),
            [VMEM, VMEM, VMEM],
        )

    for_sibling = project(1)
    sibling = in_section(for_sibling, 1, 1)
    mine = project(0)
    for_diagonal, for_across, for_direct = call(
        add_kernel,
        (shape(block, rows),) * 3,
        (mine, sibling),
        [VMEM, VMEM],
    )
    across = in_section(for_across, 1, 2)
    direct = to_encoder(for_direct)
    diagonal = lax.ppermute(
        for_diagonal, ("segment", "mp"), [(4 + i, i ^ 2) for i in range(4)]
    )
    decoder_out = call(
        final_kernel,
        shape(rows, block),
        (mine, sibling, across, residual1, direct, diagonal, from_decoder),
        [VMEM] * 7,
    )
    return decoder_out.reshape(docs, pos, block)


def solution(mesh):
    in_specs = (
        P(None, "seq", "mp"),
        P(None, "seq", "mp"),
        P("segment", None),
        P("segment", None, None, "mp"),
        P(),
    )
    out_specs = P(None, "seq", ("segment", "mp"))
    return jax.shard_map(
        on_device, mesh=mesh, in_specs=in_specs, out_specs=out_specs, check_vma=False
    )
```

```python
import functools

import jax
import jax.numpy as jnp
from jax import lax
from jax.experimental import pallas as pl
from jax.experimental.pallas import tpu as pltpu
from jax.sharding import PartitionSpec as P

DKV = 64
norm_eps = 1e-06
masked_score = -1e30
PAIR = 2 * DKV
LANES = 128
STAT_LANES = 128
CHUNKS = 8
IN_FLIGHT = 99
VMEM = pl.BlockSpec(memory_space=pltpu.VMEM)
SMEM = pl.BlockSpec(memory_space=pltpu.SMEM)
ANY = pl.BlockSpec(memory_space=pl.ANY)
f32 = jnp.float32
bf16 = jnp.bfloat16


def params():
    return pltpu.CompilerParams(vmem_limit_bytes=40 * 1024 * 1024)


def position():
    m = lax.axis_index("mp")
    return (
        lax.axis_index("segment"),
        lax.axis_index("seq"),
        m,
        m ^ 1,
        m ^ 2,
        m ^ 3,
        m & 1,
        m ^ (m >> 1),
        m ^ (2 + (m >> 1)),
    )


def squares(parts):
    return sum(jnp.sum(jnp.square(part.astype(f32)), axis=1, keepdims=True) for part in parts)


def gained(rows, inverse, gains, block):
    width = rows.shape[1]
    gain = gains[:, pl.ds(pl.multiple_of(block * width, width), width)].astype(f32)
    return (rows.astype(f32) * inverse * gain).astype(bf16)


class WeightStream:
    def __init__(self, weights, order, width, wbuf, sem):
        height = wbuf.shape[1]
        self.copies = [
            pltpu.make_async_copy(
                weights.at[0, which, pl.ds(block * width + start, height), :],
                wbuf.at[i],
                sem.at[i],
            )
            for i, (which, block, start) in enumerate(
                (which, block, start)
                for which, block in order
                for start in range(0, width, height)
            )
        ]
        self.wbuf = wbuf
        self.started = self.used = 0
        for _ in range(IN_FLIGHT):
            self.start()

    def start(self):
        if self.started < len(self.copies):
            self.copies[self.started].start()
            self.started += 1

    def product(self, rows):
        height = self.wbuf.shape[1]
        total = None
        for start in range(0, rows.shape[1], height):
            self.copies[self.used].wait()
            self.start()
            term = jnp.dot(
                rows[:, start : start + height], self.wbuf[self.used], preferred_element_type=f32
            )
            total = term if total is None else total + term
            self.used += 1
        return total


def normed_rows(parts, gains, blocks):
    inverse = lax.rsqrt(squares(parts) / gains.shape[1] + norm_eps)
    return [gained(part, inverse, gains, block) for part, block in zip(parts, blocks)]


def streamed_product(rows, stream):
    return sum(stream.product(part) for part in rows)


def near_copy_kernel(dec, gains, dec_out, gains_out):
    dec_out[...] = dec[...]
    gains_out[...] = gains[...]


def query_kernel(x0, x1, x2, x3, gains, weights, first_out, second_out, res1, wbuf, sem):
    info = position()
    blocks = info[2:6]
    rows_each = first_out.shape[0]

    @pl.when(info[0] == 1)
    def _():
        stream = WeightStream(weights, [(0, block) for block in blocks], x0.shape[1], wbuf, sem)
        half = res1.shape[1]
        offset = pl.multiple_of(info[6] * half, half)
        for k, part in enumerate((x0, x1, x2, x3)):

            @pl.when(info[7] == k)
            def _():
                for doc in range(part.shape[0] // rows_each):
                    second_out[rows_each:, doc * half : (doc + 1) * half] = part[
                        doc * rows_each : (doc + 1) * rows_each, pl.ds(offset, half)
                    ]

            @pl.when(info[8] == k)
            def _():
                res1[...] = part[:, pl.ds(offset, half)]

        parts = (x0[...], x1[...], x2[...], x3[...])
        total = streamed_product(normed_rows(parts, gains, blocks), stream)
        first_out[...] = total[:rows_each].astype(bf16)
        second_out[:rows_each] = total[rows_each:].astype(bf16)


def memory_kernel(doc, matrices, x0, x1, x2, x3, gains, weights, out, wbuf, sem):
    info = position()
    blocks = info[2:6]
    span = x2.shape[0]
    here = slice(doc * span, (doc + 1) * span)

    @pl.when(info[0] == 0)
    def _():
        order = [(which, block) for which in matrices for block in blocks]
        stream = WeightStream(weights, order, x2.shape[1], wbuf, sem)
        parts = (x0[here], x1[here], x2[...], x3[...])
        rows = normed_rows(parts, gains, blocks)
        for i in range(len(matrices)):
            out[i] = streamed_product(rows, stream).astype(bf16)


def first_memory_kernel(x0, x1, x2, x3, gains, key_weights, weights, out, wbuf, sem):
    info = position()
    blocks = info[2:6]
    span, width = x2.shape

    @pl.when(info[0] == 0)
    def _():
        stream = WeightStream(weights, [(1, block) for block in blocks], width, wbuf, sem)
        rows = normed_rows((x0[...], x1[:span], x2[...], x3[...]), gains, blocks)
        total = None
        for part, block in zip(rows, blocks):
            matrix = key_weights[pl.ds(pl.multiple_of(block * width, width), width), :]
            term = jnp.dot(part, matrix, preferred_element_type=f32)
            total = term if total is None else total + term
        out[0] = total.astype(bf16)
        out[1] = streamed_product(rows, stream).astype(bf16)


def attention_kernel(count, lengths, *refs):
    info = position()
    for side in range(2):

        @pl.when(info[0] == side)
        def _():
            attend(
                lengths[1 - side],
                info[1],
                refs[:count],
                refs[count + side],
                refs[count + 2 :],
            )


def attend(length, seq, q_refs, key_values, outs):
    count = len(q_refs)
    keys, values = (key_values.at[0], key_values.at[1])
    span = keys.shape[0]
    pos, head_width = q_refs[0].shape
    group = min(4, count)
    rows_here = group * pos
    first = seq * span
    lane = lax.broadcasted_iota(jnp.int32, (1, PAIR), 1)
    low = lane < DKV
    valid = first + lax.broadcasted_iota(jnp.int32, (1, span), 1) < length
    for base in range(0, count, group):
        stats = jnp.zeros((rows_here, STAT_LANES), f32)
        for pair in range(head_width // PAIR):
            cols = slice(pair * PAIR, (pair + 1) * PAIR)
            rows = jnp.concatenate([q_refs[base + j][:, cols] for j in range(group)], axis=0)
            zero = jnp.zeros_like(rows)
            both = jnp.concatenate(
                [jnp.where(low, rows, zero), jnp.where(low, zero, rows)], axis=0
            )
            scores = lax.dot_general(
                both, keys[:, cols], (((1,), (1,)), ((), ())), preferred_element_type=f32
            )
            masked = jnp.where(valid, scores, masked_score)
            top = jnp.max(masked, axis=1, keepdims=True)
            probs = jnp.exp(masked - top)
            total = jnp.sum(probs, axis=1, keepdims=True)
            summed = jnp.dot(probs.astype(bf16), values[:, cols], preferred_element_type=f32)
            scaled = summed * (1.0 / total)
            lse = jnp.where(first < length, top + jnp.log(total), masked_score)
            context = jnp.where(low, scaled[:rows_here], scaled[rows_here:]).astype(bf16)
            for j in range(group):
                outs[base + j][:, cols] = context[j * pos : (j + 1) * pos]
            stats = jnp.where(lane == 2 * pair, lse[:rows_here], stats)
            stats = jnp.where(lane == 2 * pair + 1, lse[rows_here:], stats)
        heads = head_width // DKV
        high = stats.astype(bf16).astype(f32)
        middle = (stats - high).astype(bf16).astype(f32)
        rest = stats - high - middle
        packed = high + pltpu.roll(middle, heads, 1) + pltpu.roll(rest, 2 * heads, 1)
        for j in range(group):
            outs[base + j][:, head_width:] = packed[j * pos : (j + 1) * pos].astype(bf16)


def combine_kernel(section, *refs):
    @pl.when(position()[0] == section)
    def _():
        combine(refs[:-1], refs[-1])


def combine(sources, out):
    head_width = out.shape[1]
    heads = head_width // DKV
    low = lax.broadcasted_iota(jnp.int32, (1, PAIR), 1) < DKV
    lses = []
    for source in sources:
        packed = source[:, head_width:].astype(f32)
        lses.append(
            packed
            + pltpu.roll(packed, STAT_LANES - heads, 1)
            + pltpu.roll(packed, STAT_LANES - 2 * heads, 1)
        )
    top = functools.reduce(jnp.maximum, lses)
    shares = [jnp.exp(lse - top) for lse in lses]
    inverse = 1.0 / sum(shares)
    shares = [share * inverse for share in shares]
    for pair in range(heads // 2):
        cols = slice(pair * PAIR, (pair + 1) * PAIR)
        context = sum(
            source[:, cols].astype(f32)
            * jnp.where(low, share[:, 2 * pair : 2 * pair + 1], share[:, 2 * pair + 1 : 2 * pair + 2])
            for source, share in zip(sources, shares)
        )
        out[:, cols] = context.astype(bf16)


def load_kernel(section, which, weights, before, out, sem):
    info = position()

    @pl.when(info[0] == section)
    def _():
        height = out.shape[0] // 8
        copies = [
            pltpu.make_async_copy(
                weights.at[0, which, pl.ds(i * height, height), :],
                out.at[pl.ds(i * height, height), :],
                sem.at[i],
            )
            for i in range(8)
        ]
        for copy in copies:
            copy.start()
        for copy in copies:
            copy.wait()


def project_kernel(mask, first_context, second_context, weights, out):
    info = position()
    block = out.shape[0] // 4
    targets = [(mask ^ 2, 0), (mask ^ 2, 4), (mask, 0), (mask, 4)]

    @pl.when(info[0] == 1)
    def _():
        context = jnp.concatenate([first_context[...], second_context[...]], axis=0)
        for i, (k, add) in enumerate(targets):
            start = pl.multiple_of((info[2 + k] + add) * block, block)
            out[i * block : (i + 1) * block, :] = lax.dot_general(
                weights[pl.ds(start, block), :],
                context,
                (((1,), (1,)), ((), ())),
                preferred_element_type=f32,
            ).astype(bf16)


def add_kernel(mine, other, *outs):
    info = position()

    @pl.when(info[0] == 1)
    def _():
        rows = outs[0].shape[0]
        for i, out in enumerate(outs):
            part = slice(i * rows, (i + 1) * rows)
            out[...] = (mine[part].astype(f32) + other[part].astype(f32)).astype(bf16)


def final_kernel(mine, sibling, across, residual1, direct, diagonal, residual0, out):
    info = position()
    block = out.shape[1]

    @pl.when(info[0] == 1)
    def _():
        part = slice(3 * block, 4 * block)
        update = mine[part].astype(f32) + sibling[part].astype(f32) + across[...].astype(f32)
        out[...] = (residual1[...].astype(f32) + update.T).astype(bf16)

    @pl.when(info[0] == 0)
    def _():
        update = direct[...].astype(f32) + diagonal[...].astype(f32)
        update = update.T
        pos = residual0.shape[0] // 2
        for doc in range(out.shape[0] // pos):
            here = slice(doc * pos, (doc + 1) * pos)
            residual = residual0[pos:, doc * block : (doc + 1) * block].astype(f32)
            out[here] = (residual + update[here]).astype(bf16)


def call(kernel, out_shapes, args, specs, scratch=(), out_specs=None, flops=1, **more):
    return pl.pallas_call(
        kernel,
        out_shape=out_shapes,
        in_specs=specs,
        out_specs=out_specs if out_specs is not None else jax.tree.map(lambda _: VMEM, out_shapes),
        scratch_shapes=list(scratch),
        compiler_params=params(),
        cost_estimate=pl.CostEstimate(flops=flops, bytes_accessed=1, transcendentals=0),
        **more,
    )(*args)


def on_device(memory, decoder_rows, gains, weights, lengths):
    segment = lax.axis_index("segment")
    seq = lax.axis_index("seq")
    m = lax.axis_index("mp")
    count = lax.axis_size("seq")
    docs, span, width = memory.shape
    pos = decoder_rows.shape[1]
    rows = docs * pos
    head_width = weights.shape[3]

    lengths = lengths.astype(jnp.int32)
    shape = lambda *dims: jax.ShapeDtypeStruct(dims, bf16)
    after = lax.optimization_barrier

    def in_section(array, section, mask):
        pairs = [(section * 4 + i, section * 4 + (i ^ mask)) for i in range(4)]
        return lax.ppermute(array, ("segment", "mp"), pairs)

    def along_seq(array, by):
        return lax.ppermute(array, "seq", [(i, (i + by) % count) for i in range(count)])

    def to_encoder(array):
        return lax.ppermute(array, "segment", [(1, 0)])

    def to_decoder(array):
        return lax.ppermute(array, "segment", [(0, 1)])

    dec = decoder_rows.reshape(rows, width)
    dec_y = in_section(dec, 1, 2)
    dec_c = in_section(dec, 1, 1)
    extra = span * 64 // 256
    first_rows, memory = after((memory[0], memory))
    mem = memory.reshape(docs * span, width)
    mem_y = [in_section(first_rows, 0, 2), in_section(mem[span - extra :], 0, 2)]
    mem_c = in_section(mem, 0, 1)

    def weight_scratch(matrices):
        chunks = matrices * CHUNKS
        return [
            pltpu.VMEM((chunks, 4 * width // CHUNKS, head_width), bf16),
            pltpu.SemaphoreType.DMA((chunks,)),
        ]

    dec_here, gains = call(
        near_copy_kernel, (shape(rows, width), shape(*gains.shape)), (dec, gains), [VMEM] * 2
    )
    dec_y, _ = after((dec_y, gains))
    dec_yc = in_section(dec_y, 1, 1)
    first_queries, for_encoder, residual1 = call(
        query_kernel,
        (shape(pos, head_width), shape(2 * pos, head_width), shape(rows, width // 2)),
        (dec_here, dec_c, dec_y, dec_yc, gains, weights),
        [VMEM] * 5 + [ANY],
        weight_scratch(1),
    )
    from_decoder = to_encoder(for_encoder)

    def project_memory(doc, matrices, far, far_c, cost):
        return call(
            functools.partial(memory_kernel, doc, matrices),
            shape(len(matrices), span, head_width),
            (mem, mem_c, far, far_c, gains, weights),
            [VMEM] * 5 + [ANY],
            weight_scratch(len(matrices)),
            flops=int(cost),
        )

    def load(section, which, before):
        return call(
            functools.partial(load_kernel, section, which),
            shape(4 * width, head_width),
            (weights, before),
            [ANY, ANY],
            [pltpu.SemaphoreType.DMA((8,))],
        )

    key_weights = load(0, 0, for_encoder)
    far, _ = after((mem_y[0], key_weights))
    far_c = in_section(far, 0, 1)
    made = call(
        first_memory_kernel,
        shape(2, span, head_width),
        (first_rows, mem_c, far, far_c, gains, key_weights, weights),
        [VMEM] * 6 + [ANY],
        weight_scratch(1),
    )
    first_memory = to_decoder(made)
    from_decoder, _ = after((from_decoder, made))
    far, _ = after((mem_y[1], from_decoder))
    far = far[extra:]
    second_memory = project_memory(1, (0, 1), far, in_section(far, 0, 1), 4.8e9)

    encoding = segment == 0
    q_pieces = [jnp.where(encoding, from_decoder[:pos], first_queries)]
    for by in range(1, count):
        q_pieces.append(along_seq(q_pieces[0], by))

    partial = call(
        functools.partial(attention_kernel, count),
        (shape(pos, head_width + STAT_LANES),) * count,
        (lengths, *q_pieces, second_memory, first_memory),
        [SMEM] + [VMEM] * (count + 2),
    )
    sources = [partial[0]] + [along_seq(partial[by], -by) for by in range(1, count)]
    def combined(section, sources):
        return call(
            functools.partial(combine_kernel, section),
            shape(pos, head_width),
            tuple(sources),
            [VMEM] * count,
        )

    second_context = combined(0, sources)
    sources[0], _ = after((sources[0], second_context))
    context = combined(1, sources)
    second_context = to_decoder(second_context)

    last_weights = load(1, 1, context)
    block = 4 * width // 8

    def project(mask):
        return call(
            functools.partial(project_kernel, mask),
            shape(4 * block, rows),
            (context, second_context, last_weights),
            [VMEM, VMEM, VMEM],
        )

    for_sibling = project(1)
    sibling = in_section(for_sibling, 1, 1)
    mine = project(0)
    for_diagonal, for_across, for_direct = call(
        add_kernel,
        (shape(block, rows),) * 3,
        (mine, sibling),
        [VMEM, VMEM],
    )
    across = in_section(for_across, 1, 2)
    direct = to_encoder(for_direct)
    diagonal = lax.ppermute(
        for_diagonal, ("segment", "mp"), [(4 + i, i ^ 2) for i in range(4)]
    )
    decoder_out = call(
        final_kernel,
        shape(rows, block),
        (mine, sibling, across, residual1, direct, diagonal, from_decoder),
        [VMEM] * 7,
    )
    return decoder_out.reshape(docs, pos, block)


def solution(mesh):
    in_specs = (
        P(None, "seq", "mp"),
        P(None, "seq", "mp"),
        P("segment", None),
        P("segment", None, None, "mp"),
        P(),
    )
    out_specs = P(None, "seq", ("segment", "mp"))
    return jax.shard_map(
        on_device, mesh=mesh, in_specs=in_specs, out_specs=out_specs, check_vma=False
    )
```

```python
import functools

import jax
import jax.numpy as jnp
from jax import lax
from jax.experimental import pallas as pl
from jax.experimental.pallas import tpu as pltpu
from jax.sharding import PartitionSpec as P

DKV = 64
norm_eps = 1e-06
masked_score = -1e30
PAIR = 2 * DKV
LANES = 128
STAT_LANES = 128
CHUNKS = 8
IN_FLIGHT = 99
VMEM = pl.BlockSpec(memory_space=pltpu.VMEM)
SMEM = pl.BlockSpec(memory_space=pltpu.SMEM)
ANY = pl.BlockSpec(memory_space=pl.ANY)
f32 = jnp.float32
bf16 = jnp.bfloat16


def params():
    return pltpu.CompilerParams(vmem_limit_bytes=40 * 1024 * 1024)


def position():
    m = lax.axis_index("mp")
    return (
        lax.axis_index("segment"),
        lax.axis_index("seq"),
        m,
        m ^ 1,
        m ^ 2,
        m ^ 3,
        m & 1,
        m ^ (m >> 1),
        m ^ (2 + (m >> 1)),
    )


def squares(parts):
    return sum(jnp.sum(jnp.square(part.astype(f32)), axis=1, keepdims=True) for part in parts)


def gained(rows, inverse, gains, block):
    width = rows.shape[1]
    gain = gains[:, pl.ds(pl.multiple_of(block * width, width), width)].astype(f32)
    return (rows.astype(f32) * inverse * gain).astype(bf16)


class WeightStream:
    def __init__(self, weights, order, width, wbuf, sem):
        height = wbuf.shape[1]
        self.copies = [
            pltpu.make_async_copy(
                weights.at[0, which, pl.ds(block * width + start, height), :],
                wbuf.at[i],
                sem.at[i],
            )
            for i, (which, block, start) in enumerate(
                (which, block, start)
                for which, block in order
                for start in range(0, width, height)
            )
        ]
        self.wbuf = wbuf
        self.started = self.used = 0
        for _ in range(IN_FLIGHT):
            self.start()

    def start(self):
        if self.started < len(self.copies):
            self.copies[self.started].start()
            self.started += 1

    def product(self, rows):
        height = self.wbuf.shape[1]
        total = None
        for start in range(0, rows.shape[1], height):
            self.copies[self.used].wait()
            self.start()
            term = jnp.dot(
                rows[:, start : start + height], self.wbuf[self.used], preferred_element_type=f32
            )
            total = term if total is None else total + term
            self.used += 1
        return total


def normed_rows(parts, gains, blocks):
    inverse = lax.rsqrt(squares(parts) / gains.shape[1] + norm_eps)
    return [gained(part, inverse, gains, block) for part, block in zip(parts, blocks)]


def streamed_product(rows, stream):
    return sum(stream.product(part) for part in rows)


def near_copy_kernel(dec, gains, dec_out, gains_out):
    dec_out[...] = dec[...]
    gains_out[...] = gains[...]


def query_kernel(x0, x1, x2, x3, gains, weights, first_out, second_out, res1, wbuf, sem):
    info = position()
    blocks = info[2:6]
    rows_each = first_out.shape[0]

    @pl.when(info[0] == 1)
    def _():
        stream = WeightStream(weights, [(0, block) for block in blocks], x0.shape[1], wbuf, sem)
        half = res1.shape[1]
        offset = pl.multiple_of(info[6] * half, half)
        for k, part in enumerate((x0, x1, x2, x3)):

            @pl.when(info[7] == k)
            def _():
                for doc in range(part.shape[0] // rows_each):
                    second_out[rows_each:, doc * half : (doc + 1) * half] = part[
                        doc * rows_each : (doc + 1) * rows_each, pl.ds(offset, half)
                    ]

            @pl.when(info[8] == k)
            def _():
                res1[...] = part[:, pl.ds(offset, half)]

        parts = (x0[...], x1[...], x2[...], x3[...])
        total = streamed_product(normed_rows(parts, gains, blocks), stream)
        first_out[...] = total[:rows_each].astype(bf16)
        second_out[:rows_each] = total[rows_each:].astype(bf16)


def memory_kernel(doc, matrices, x0, x1, x2, x3, gains, weights, out, wbuf, sem):
    info = position()
    blocks = info[2:6]
    span = x2.shape[0]
    here = slice(doc * span, (doc + 1) * span)

    @pl.when(info[0] == 0)
    def _():
        order = [(which, block) for which in matrices for block in blocks]
        stream = WeightStream(weights, order, x2.shape[1], wbuf, sem)
        parts = (x0[here], x1[here], x2[...], x3[...])
        rows = normed_rows(parts, gains, blocks)
        for i in range(len(matrices)):
            out[i] = streamed_product(rows, stream).astype(bf16)


def first_memory_kernel(x0, x1, x2, x3, gains, key_weights, weights, out, wbuf, sem):
    info = position()
    blocks = info[2:6]
    span, width = x2.shape

    @pl.when(info[0] == 0)
    def _():
        stream = WeightStream(weights, [(1, block) for block in blocks], width, wbuf, sem)
        rows = normed_rows((x0[...], x1[:span], x2[...], x3[...]), gains, blocks)
        total = None
        for part, block in zip(rows, blocks):
            matrix = key_weights[pl.ds(pl.multiple_of(block * width, width), width), :]
            term = jnp.dot(part, matrix, preferred_element_type=f32)
            total = term if total is None else total + term
        out[0] = total.astype(bf16)
        out[1] = streamed_product(rows, stream).astype(bf16)


def attention_kernel(count, lengths, *refs):
    info = position()
    for side in range(2):

        @pl.when(info[0] == side)
        def _():
            attend(
                lengths[1 - side],
                info[1],
                refs[:count],
                refs[count + side],
                refs[count + 2 :],
            )


def attend(length, seq, q_refs, key_values, outs):
    count = len(q_refs)
    keys, values = (key_values.at[0], key_values.at[1])
    span = keys.shape[0]
    pos, head_width = q_refs[0].shape
    group = min(4, count)
    rows_here = group * pos
    first = seq * span
    lane = lax.broadcasted_iota(jnp.int32, (1, PAIR), 1)
    low = lane < DKV
    valid = first + lax.broadcasted_iota(jnp.int32, (1, span), 1) < length
    for base in range(0, count, group):
        stats = jnp.zeros((rows_here, STAT_LANES), f32)
        for pair in range(head_width // PAIR):
            cols = slice(pair * PAIR, (pair + 1) * PAIR)
            rows = jnp.concatenate([q_refs[base + j][:, cols] for j in range(group)], axis=0)
            zero = jnp.zeros_like(rows)
            both = jnp.concatenate(
                [jnp.where(low, rows, zero), jnp.where(low, zero, rows)], axis=0
            )
            scores = lax.dot_general(
                both, keys[:, cols], (((1,), (1,)), ((), ())), preferred_element_type=f32
            )
            masked = jnp.where(valid, scores, masked_score)
            top = jnp.max(masked, axis=1, keepdims=True)
            probs = jnp.exp(masked - top)
            total = jnp.sum(probs, axis=1, keepdims=True)
            summed = jnp.dot(probs.astype(bf16), values[:, cols], preferred_element_type=f32)
            scaled = summed * (1.0 / total)
            lse = jnp.where(first < length, top + jnp.log(total), masked_score)
            context = jnp.where(low, scaled[:rows_here], scaled[rows_here:]).astype(bf16)
            for j in range(group):
                outs[base + j][:, cols] = context[j * pos : (j + 1) * pos]
            stats = jnp.where(lane == 2 * pair, lse[:rows_here], stats)
            stats = jnp.where(lane == 2 * pair + 1, lse[rows_here:], stats)
        heads = head_width // DKV
        high = stats.astype(bf16).astype(f32)
        middle = (stats - high).astype(bf16).astype(f32)
        rest = stats - high - middle
        packed = high + pltpu.roll(middle, heads, 1) + pltpu.roll(rest, 2 * heads, 1)
        for j in range(group):
            outs[base + j][:, head_width:] = packed[j * pos : (j + 1) * pos].astype(bf16)


def combine_kernel(section, *refs):
    @pl.when(position()[0] == section)
    def _():
        combine(refs[:-1], refs[-1])


def combine(sources, out):
    head_width = out.shape[1]
    heads = head_width // DKV
    low = lax.broadcasted_iota(jnp.int32, (1, PAIR), 1) < DKV
    lses = []
    for source in sources:
        packed = source[:, head_width:].astype(f32)
        lses.append(
            packed
            + pltpu.roll(packed, STAT_LANES - heads, 1)
            + pltpu.roll(packed, STAT_LANES - 2 * heads, 1)
        )
    top = functools.reduce(jnp.maximum, lses)
    shares = [jnp.exp(lse - top) for lse in lses]
    inverse = 1.0 / sum(shares)
    shares = [share * inverse for share in shares]
    for pair in range(heads // 2):
        cols = slice(pair * PAIR, (pair + 1) * PAIR)
        context = sum(
            source[:, cols].astype(f32)
            * jnp.where(low, share[:, 2 * pair : 2 * pair + 1], share[:, 2 * pair + 1 : 2 * pair + 2])
            for source, share in zip(sources, shares)
        )
        out[:, cols] = context.astype(bf16)


def load_kernel(section, which, weights, before, out, sem):
    info = position()

    @pl.when(info[0] == section)
    def _():
        height = out.shape[0] // 8
        copies = [
            pltpu.make_async_copy(
                weights.at[0, which, pl.ds(i * height, height), :],
                out.at[pl.ds(i * height, height), :],
                sem.at[i],
            )
            for i in range(8)
        ]
        for copy in copies:
            copy.start()
        for copy in copies:
            copy.wait()


def project_kernel(mask, first_context, second_context, weights, out):
    info = position()
    block = out.shape[0] // 4
    targets = [(mask ^ 2, 0), (mask ^ 2, 4), (mask, 0), (mask, 4)]

    @pl.when(info[0] == 1)
    def _():
        context = jnp.concatenate([first_context[...], second_context[...]], axis=0)
        for i, (k, add) in enumerate(targets):
            start = pl.multiple_of((info[2 + k] + add) * block, block)
            out[i * block : (i + 1) * block, :] = lax.dot_general(
                weights[pl.ds(start, block), :],
                context,
                (((1,), (1,)), ((), ())),
                preferred_element_type=f32,
            ).astype(bf16)


def add_kernel(mine, other, *outs):
    info = position()

    @pl.when(info[0] == 1)
    def _():
        rows = outs[0].shape[0]
        for i, out in enumerate(outs):
            part = slice(i * rows, (i + 1) * rows)
            out[...] = (mine[part].astype(f32) + other[part].astype(f32)).astype(bf16)


def final_kernel(mine, sibling, across, residual1, direct, diagonal, residual0, out):
    info = position()
    block = out.shape[1]

    @pl.when(info[0] == 1)
    def _():
        part = slice(3 * block, 4 * block)
        update = mine[part].astype(f32) + sibling[part].astype(f32) + across[...].astype(f32)
        out[...] = (residual1[...].astype(f32) + update.T).astype(bf16)

    @pl.when(info[0] == 0)
    def _():
        update = direct[...].astype(f32) + diagonal[...].astype(f32)
        update = update.T
        pos = residual0.shape[0] // 2
        for doc in range(out.shape[0] // pos):
            here = slice(doc * pos, (doc + 1) * pos)
            residual = residual0[pos:, doc * block : (doc + 1) * block].astype(f32)
            out[here] = (residual + update[here]).astype(bf16)


def call(kernel, out_shapes, args, specs, scratch=(), out_specs=None, flops=1, **more):
    return pl.pallas_call(
        kernel,
        out_shape=out_shapes,
        in_specs=specs,
        out_specs=out_specs if out_specs is not None else jax.tree.map(lambda _: VMEM, out_shapes),
        scratch_shapes=list(scratch),
        compiler_params=params(),
        cost_estimate=pl.CostEstimate(flops=flops, bytes_accessed=1, transcendentals=0),
        **more,
    )(*args)


def on_device(memory, decoder_rows, gains, weights, lengths):
    segment = lax.axis_index("segment")
    seq = lax.axis_index("seq")
    m = lax.axis_index("mp")
    count = lax.axis_size("seq")
    docs, span, width = memory.shape
    pos = decoder_rows.shape[1]
    rows = docs * pos
    head_width = weights.shape[3]

    lengths = lengths.astype(jnp.int32)
    shape = lambda *dims: jax.ShapeDtypeStruct(dims, bf16)
    after = lax.optimization_barrier

    def in_section(array, section, mask):
        pairs = [(section * 4 + i, section * 4 + (i ^ mask)) for i in range(4)]
        return lax.ppermute(array, ("segment", "mp"), pairs)

    def along_seq(array, by):
        return lax.ppermute(array, "seq", [(i, i ^ by) for i in range(count)])

    def to_encoder(array):
        return lax.ppermute(array, "segment", [(1, 0)])

    def to_decoder(array):
        return lax.ppermute(array, "segment", [(0, 1)])

    dec = decoder_rows.reshape(rows, width)
    dec_y = in_section(dec, 1, 2)
    dec_c = in_section(dec, 1, 1)
    extra = span * 64 // 256
    first_rows, memory = after((memory[0], memory))
    mem = memory.reshape(docs * span, width)
    mem_y = [in_section(first_rows, 0, 2), in_section(mem[span - extra :], 0, 2)]
    mem_c = in_section(mem, 0, 1)

    def weight_scratch(matrices):
        chunks = matrices * CHUNKS
        return [
            pltpu.VMEM((chunks, 4 * width // CHUNKS, head_width), bf16),
            pltpu.SemaphoreType.DMA((chunks,)),
        ]

    dec_here, gains = call(
        near_copy_kernel, (shape(rows, width), shape(*gains.shape)), (dec, gains), [VMEM] * 2
    )
    dec_y, _ = after((dec_y, gains))
    dec_yc = in_section(dec_y, 1, 1)
    first_queries, for_encoder, residual1 = call(
        query_kernel,
        (shape(pos, head_width), shape(2 * pos, head_width), shape(rows, width // 2)),
        (dec_here, dec_c, dec_y, dec_yc, gains, weights),
        [VMEM] * 5 + [ANY],
        weight_scratch(1),
    )
    from_decoder = to_encoder(for_encoder)

    def project_memory(doc, matrices, far, far_c, cost):
        return call(
            functools.partial(memory_kernel, doc, matrices),
            shape(len(matrices), span, head_width),
            (mem, mem_c, far, far_c, gains, weights),
            [VMEM] * 5 + [ANY],
            weight_scratch(len(matrices)),
            flops=int(cost),
        )

    def load(section, which, before):
        return call(
            functools.partial(load_kernel, section, which),
            shape(4 * width, head_width),
            (weights, before),
            [ANY, ANY],
            [pltpu.SemaphoreType.DMA((8,))],
        )

    key_weights = load(0, 0, for_encoder)
    far, _ = after((mem_y[0], key_weights))
    far_c = in_section(far, 0, 1)
    made = call(
        first_memory_kernel,
        shape(2, span, head_width),
        (first_rows, mem_c, far, far_c, gains, key_weights, weights),
        [VMEM] * 6 + [ANY],
        weight_scratch(1),
    )
    first_memory = to_decoder(made)
    from_decoder, _ = after((from_decoder, made))
    far, _ = after((mem_y[1], from_decoder))
    far = far[extra:]
    second_memory = project_memory(1, (0, 1), far, in_section(far, 0, 1), 4.8e9)

    encoding = segment == 0
    q_pieces = [jnp.where(encoding, from_decoder[:pos], first_queries)]
    for by in range(1, count):
        q_pieces.append(along_seq(q_pieces[0], by))

    partial = call(
        functools.partial(attention_kernel, count),
        (shape(pos, head_width + STAT_LANES),) * count,
        (lengths, *q_pieces, second_memory, first_memory),
        [SMEM] + [VMEM] * (count + 2),
    )
    order = sorted(range(1, count), key=lambda by: by == 1)
    sources = [partial[0]] + [along_seq(partial[by], by) for by in order]
    def combined(section, sources):
        return call(
            functools.partial(combine_kernel, section),
            shape(pos, head_width),
            tuple(sources),
            [VMEM] * count,
        )

    second_context = combined(0, sources)
    sources[0], _ = after((sources[0], second_context))
    context = combined(1, sources)
    second_context = to_decoder(second_context)

    last_weights = load(1, 1, context)
    block = 4 * width // 8

    def project(mask):
        return call(
            functools.partial(project_kernel, mask),
            shape(4 * block, rows),
            (context, second_context, last_weights),
            [VMEM, VMEM, VMEM],
        )

    for_sibling = project(1)
    sibling = in_section(for_sibling, 1, 1)
    mine = project(0)
    for_diagonal, for_across, for_direct = call(
        add_kernel,
        (shape(block, rows),) * 3,
        (mine, sibling),
        [VMEM, VMEM],
    )
    across = in_section(for_across, 1, 2)
    direct = to_encoder(for_direct)
    diagonal = lax.ppermute(
        for_diagonal, ("segment", "mp"), [(4 + i, i ^ 2) for i in range(4)]
    )
    decoder_out = call(
        final_kernel,
        shape(rows, block),
        (mine, sibling, across, residual1, direct, diagonal, from_decoder),
        [VMEM] * 7,
    )
    return decoder_out.reshape(docs, pos, block)


def solution(mesh):
    in_specs = (
        P(None, "seq", "mp"),
        P(None, "seq", "mp"),
        P("segment", None),
        P("segment", None, None, "mp"),
        P(),
    )
    out_specs = P(None, "seq", ("segment", "mp"))
    return jax.shard_map(
        on_device, mesh=mesh, in_specs=in_specs, out_specs=out_specs, check_vma=False
    )
```
